32 devices in a mesh: seq: 16 (over z, y, x), head: 2 (over core).
Axes of the slice: x: 2, y: 2, z: 4, core: 2. Of those that a mesh axis runs over, the one named last changes fastest.
Arguments:
- queries: bfloat16 [512, 4096], P('seq', 'head'), may hold values from -6 to 6
- cache_keys: bfloat16 [65536, 1024], P('seq', 'head'), may hold values from -8 to 8
- cache_values: bfloat16 [65536, 1024], P('seq', 'head'), may hold values from -8 to 8
- new_keys: bfloat16 [512, 1024], P('seq', 'head'), may hold values from -8 to 8
- new_values: bfloat16 [512, 1024], P('seq', 'head'), may hold values from -8 to 8
- new_pos: int32 [512], replicated, may hold values from 0 to 511, as said below
- residual: bfloat16 [512, 4096], P('head', 'seq'), may hold values from -6 to 6
- out_weight: bfloat16 [4096, 4096], P('head', 'seq'), may hold values from -0.09375 to 0.09375
Outputs:
- attended: bfloat16 [512, 4096], P('seq', 'head')
- hidden: bfloat16 [512, 4096], P('head', 'seq')
The draws below stay inside these ranges and needn't reach their ends.
Inputs may be any that keep to these rules, and one draw needn't show every extreme that they name: `new_pos`: each number of 0 to 511 appears exactly once.
All inputs are finite; a program needn't handle non-finite values.
Results may differ from the reference program's by a relative error of at most 0.0095.
Values may be sent and summed in bfloat16 or wider, within the bound.
A program may use at most 128 MiB of HBM per device.

```python
import math
import jax
import jax.numpy as jnp
from jax import lax

D = 4096
HQ = 32
KVH = 8
HD = 128
TURN = 128
NEW = 512
PREFIX = 65536


def common_parts(key):
    token_order = jax.random.permutation(jax.random.fold_in(key, 101), NEW).astype(jnp.int32)
    base_draw = jax.random.normal(jax.random.fold_in(key, 102), (NEW, HQ * HD), jnp.float32)
    return (token_order, base_draw)


def scaled_queries(base_draw):
    return jnp.clip(1.5 * base_draw, -6.0, 6.0)


def draw_queries(key, part):
    token_order, base_draw = common_parts(key)
    values = scaled_queries(base_draw)
    return values.astype(jnp.bfloat16)


def draw_new_keys(key, part):
    token_order, base_draw = common_parts(key)
    key = jax.random.fold_in(key, 2)
    query_like = scaled_queries(base_draw)
    leading = query_like.reshape(NEW, KVH, HQ // KVH, HD)[:, :, 0, :].reshape(NEW, KVH * HD)
    noise_part = 1.2 * jax.random.normal(key, (NEW, KVH * HD), jnp.float32)
    return jnp.clip(0.65 * leading + noise_part, -8.0, 8.0).astype(jnp.bfloat16)


def draw_cache_keys(key, part):
    key = jax.random.fold_in(key, 3)
    values = jnp.clip(2.0 * jax.random.normal(key, (PREFIX, KVH * HD), jnp.float32), -8.0, 8.0)
    return values.astype(jnp.bfloat16)


def draw_new_pos(key, part):
    token_order, base_draw = common_parts(key)
    return token_order


def levels(own_key, extent, split, smallest, largest):
    level, own = 1.0, jax.random.fold_in(own_key, 6)
    for dim, shards_of in split:
        steps = jnp.exp(jax.random.uniform(jax.random.fold_in(own, dim), (shards_of,), jnp.float32, smallest / len(split), largest / len(split)))
        level = level * jnp.repeat(steps, extent[dim] // shards_of).reshape([-1 if axis == dim else 1 for axis in range(len(extent))])
    return level


def bell_draw(key, shape, width, reach, cuts=(), held_as=jnp.bfloat16):
    level = levels(key, shape, cuts, -0.22, 0.18) if cuts else 1.0
    values = jax.random.normal(key, shape, jnp.float32) * width * level
    return jnp.minimum(jnp.maximum(values, -reach), reach).astype(held_as)


def setup_inputs(seed: int = 0) -> dict:
    keys = jax.random.split(jax.random.key(seed), 9)
    queries = draw_queries(jax.random.fold_in(keys[8], 71), 0)
    cache_keys = draw_cache_keys(jax.random.fold_in(keys[8], 71), 0)
    cache_values = bell_draw(keys[2], (PREFIX, KVH * HD), 2.0, 8.0, ((0, 16), (1, 2)))
    new_keys = draw_new_keys(jax.random.fold_in(keys[8], 71), 0)
    new_values = bell_draw(keys[4], (NEW, KVH * HD), 2.0, 8.0, ((0, 16), (1, 2)))
    new_pos = draw_new_pos(jax.random.fold_in(keys[8], 71), 0)
    residual = bell_draw(keys[6], (NEW, D), 1.0, 6.0, ((0, 2), (1, 16)))
    out_weight = bell_draw(keys[7], (D, D), D ** -0.5, 0.09375, ((0, 2), (1, 16)))
    return {"queries": queries, "cache_keys": cache_keys, "cache_values": cache_values, "new_keys": new_keys, "new_values": new_values, "new_pos": new_pos, "residual": residual, "out_weight": out_weight}


rope_base = 3580165449.0

def rotate(vectors, offsets):
    half_width = vectors.shape[-1] // 2
    frequency = jnp.exp(jnp.arange(half_width, dtype=jnp.float32) * (-2.0 * math.log(rope_base) / vectors.shape[-1]))
    angles = offsets.astype(jnp.float32)[:, None] * frequency[None, :]
    cosine = jnp.concatenate([jnp.cos(angles), jnp.cos(angles)], axis=-1)[:, None, :]
    sine_part = jnp.concatenate([jnp.sin(angles), jnp.sin(angles)], axis=-1)[:, None, :]
    turned = jnp.concatenate([-vectors[..., half_width:], vectors[..., :half_width]], axis=-1)
    return vectors * cosine + turned * sine_part

def reference(queries, cache_keys, cache_values, new_keys, new_values, new_pos, residual, out_weight):
    group_size = HQ // KVH
    offsets = new_pos % TURN
    turn_ids = new_pos // TURN
    query_rot = rotate(queries.astype(jnp.float32).reshape(NEW, HQ, HD), offsets).astype(jnp.bfloat16)
    key_rot = rotate(new_keys.astype(jnp.float32).reshape(NEW, KVH, HD), offsets).astype(jnp.bfloat16)
    grouped = query_rot.reshape(NEW, KVH, group_size, HD).transpose(1, 0, 2, 3).reshape(KVH, NEW * group_size, HD).astype(jnp.float32)
    block_rows = math.gcd(PREFIX, 4096)
    block_count = PREFIX // block_rows
    key_blocks = cache_keys.reshape(block_count, block_rows, KVH, HD)
    value_blocks = cache_values.reshape(block_count, block_rows, KVH, HD)
    score_scale = 1.0 / math.sqrt(HD)

    def fold_scores(carry, scores, value_block):
        running_max, running_sum, running_out = carry
        new_max = jnp.maximum(running_max, lax.optimization_barrier(jnp.max(scores, axis=-1)))
        shrink = jnp.exp(running_max - new_max)
        exps = jnp.exp(scores - new_max[..., None])
        running_sum = running_sum * shrink + lax.optimization_barrier(jnp.sum(exps, axis=-1))
        rounded = lax.optimization_barrier(exps.astype(jnp.bfloat16)).astype(jnp.float32)
        running_out = running_out * shrink[..., None] + jnp.einsum('grk,kgd->grd', rounded, value_block)
        return (new_max, running_sum, running_out)

    def absorb(carry, blocks):
        key_block = blocks[0].astype(jnp.float32)
        value_block = blocks[1].astype(jnp.float32)
        scores = jnp.einsum('grd,kgd->grk', grouped, key_block) * score_scale
        return (fold_scores(carry, scores, value_block), None)
    start_max = jnp.full((KVH, NEW * group_size), -1e+30, jnp.float32)
    start_sum = jnp.zeros((KVH, NEW * group_size), jnp.float32)
    start_out = jnp.zeros((KVH, NEW * group_size, HD), jnp.float32)
    carry, unused = lax.scan(absorb, (start_max, start_sum, start_out), (key_blocks, value_blocks))
    visible = (turn_ids[:, None] == turn_ids[None, :]) & (offsets[None, :] <= offsets[:, None])
    visible = jnp.repeat(visible, group_size, axis=0)[None]
    scores = jnp.einsum('grd,kgd->grk', grouped, key_rot.astype(jnp.float32)) * score_scale
    masked = jnp.where(visible, scores, -1e+30)
    running_max, running_sum, running_out = carry
    new_max = jnp.maximum(running_max, lax.optimization_barrier(jnp.max(masked, axis=-1)))
    shrink = jnp.exp(running_max - new_max)
    exps = jnp.where(visible, jnp.exp(masked - new_max[..., None]), 0.0)
    running_sum = running_sum * shrink + lax.optimization_barrier(jnp.sum(exps, axis=-1))
    rounded = lax.optimization_barrier(exps.astype(jnp.bfloat16)).astype(jnp.float32)
    value_new = new_values.reshape(NEW, KVH, HD).astype(jnp.float32)
    running_out = running_out * shrink[..., None] + jnp.einsum('grk,kgd->grd', rounded, value_new)
    result = running_out / running_sum[..., None]
    attended = result.reshape(KVH, NEW, group_size, HD).transpose(1, 0, 2, 3).reshape(NEW, HQ * HD).astype(jnp.bfloat16)
    hidden = (residual.astype(jnp.float32) + jnp.dot(attended, out_weight, preferred_element_type=jnp.float32)).astype(jnp.bfloat16)
    return (attended, hidden)
```

```python
import functools
import math

import jax
import jax.numpy as jnp
from jax import lax
from jax.experimental import pallas as pl
from jax.experimental.pallas import tpu as pltpu
from jax.sharding import PartitionSpec as P

HD = 128
TURN = 128


rope_base = 3580165449.0


def rotate(vectors, offsets):
    half_width = vectors.shape[-1] // 2
    frequency = jnp.exp(
        jnp.arange(half_width, dtype=jnp.float32) * (-2.0 * math.log(rope_base) / vectors.shape[-1])
    )
    angles = offsets.astype(jnp.float32)[:, None] * frequency[None, :]
    cosine = jnp.concatenate([jnp.cos(angles), jnp.cos(angles)], axis=-1)[:, None, :]
    sine_part = jnp.concatenate([jnp.sin(angles), jnp.sin(angles)], axis=-1)[:, None, :]
    turned = jnp.concatenate([-vectors[..., half_width:], vectors[..., :half_width]], axis=-1)
    return vectors * cosine + turned * sine_part


def fold_scores(carry, scores, value_block, visible):
    running_max, running_sum, running_out = carry
    new_max = jnp.maximum(running_max, jnp.max(scores, axis=-1))
    shrink = jnp.exp(running_max - new_max)
    exps = jnp.exp(scores - new_max[..., None])
    if visible is not None:
        exps = jnp.where(visible, exps, 0.0)
    running_sum = running_sum * shrink + jnp.sum(exps, axis=-1)
    product = jnp.einsum(
        "grk,kgd->grd", exps.astype(jnp.bfloat16), value_block, preferred_element_type=jnp.float32
    )
    running_out = running_out * shrink[..., None] + product
    return (new_max, running_sum, running_out)


def plain_device(
    queries, cache_keys, cache_values, new_keys, new_values, new_pos, residual, out_weight
):
    local_rows = queries.shape[0]
    kv_local = cache_keys.shape[1] // HD
    group_size = queries.shape[1] // cache_keys.shape[1]
    offsets = new_pos % TURN
    turn_ids = new_pos // TURN
    row_start = lax.axis_index("seq") * local_rows
    own_offsets = lax.dynamic_slice_in_dim(offsets, row_start, local_rows)
    own_turns = lax.dynamic_slice_in_dim(turn_ids, row_start, local_rows)
    query_rot = rotate(
        queries.astype(jnp.float32).reshape(local_rows, kv_local * group_size, HD), own_offsets
    )
    query_rot = query_rot.astype(jnp.bfloat16).reshape(local_rows, kv_local * group_size * HD)
    key_rot = rotate(
        new_keys.astype(jnp.float32).reshape(local_rows, kv_local, HD), own_offsets
    ).astype(jnp.bfloat16)
    all_queries = lax.all_gather(query_rot, "seq", axis=0, tiled=True)
    total_rows = all_queries.shape[0]
    head_local = kv_local * group_size
    grouped = (
        all_queries.reshape(total_rows, kv_local, group_size, HD)
        .transpose(1, 0, 2, 3)
        .reshape(kv_local, total_rows * group_size, HD)
    )
    score_scale = 1.0 / math.sqrt(HD)
    block_rows = min(512, cache_keys.shape[0])
    block_count = cache_keys.shape[0] // block_rows
    key_blocks = cache_keys.reshape(block_count, block_rows, kv_local, HD)
    value_blocks = cache_values.reshape(block_count, block_rows, kv_local, HD)

    def absorb(carry, blocks):
        scores = (
            jnp.einsum("grd,kgd->grk", grouped, blocks[0], preferred_element_type=jnp.float32)
            * score_scale
        )
        return (fold_scores(carry, scores, blocks[1], None), None)

    start_max = jnp.full((kv_local, total_rows * group_size), -1e30, jnp.float32)
    start_sum = jnp.zeros((kv_local, total_rows * group_size), jnp.float32)
    start_out = jnp.zeros((kv_local, total_rows * group_size, HD), jnp.float32)
    carry, unused = lax.scan(absorb, (start_max, start_sum, start_out), (key_blocks, value_blocks))
    visible = (turn_ids[:, None] == own_turns[None, :]) & (own_offsets[None, :] <= offsets[:, None])
    visible = jnp.repeat(visible, group_size, axis=0)[None]
    scores = (
        jnp.einsum("grd,kgd->grk", grouped, key_rot, preferred_element_type=jnp.float32)
        * score_scale
    )
    masked = jnp.where(visible, scores, -1e30)
    value_new = new_values.reshape(local_rows, kv_local, HD)
    running_max, running_sum, running_out = fold_scores(carry, masked, value_new, visible)
    out_rows = (
        running_out.reshape(kv_local, total_rows, group_size, HD)
        .transpose(1, 0, 2, 3)
        .reshape(total_rows, head_local * HD)
    )
    max_rows = (
        running_max.reshape(kv_local, total_rows, group_size)
        .transpose(1, 0, 2)
        .reshape(total_rows, head_local)
    )
    sum_rows = (
        running_sum.reshape(kv_local, total_rows, group_size)
        .transpose(1, 0, 2)
        .reshape(total_rows, head_local)
    )
    partials, maxima, totals = (
        lax.all_to_all(out_rows[None], "seq", split_axis=1, concat_axis=0, tiled=True),
        lax.all_to_all(max_rows[None], "seq", split_axis=1, concat_axis=0, tiled=True),
        lax.all_to_all(sum_rows[None], "seq", split_axis=1, concat_axis=0, tiled=True),
    )
    peak_score = jnp.max(maxima, axis=0)
    weight = jnp.exp(maxima - peak_score[None])
    numerator = jnp.sum(
        partials.reshape(partials.shape[0], local_rows, head_local, HD) * weight[..., None], axis=0
    )
    denominator = jnp.sum(totals * weight, axis=0)
    attended = (
        (numerator / denominator[..., None])
        .reshape(local_rows, head_local * HD)
        .astype(jnp.bfloat16)
    )
    projected = jnp.dot(
        lax.all_gather(attended, "seq", axis=0, tiled=True),
        out_weight,
        preferred_element_type=jnp.float32,
    )
    summed = lax.psum_scatter(
        projected.astype(jnp.bfloat16), "head", scatter_dimension=0, tiled=True
    ).astype(jnp.float32)
    hidden = (residual.astype(jnp.float32) + summed).astype(jnp.bfloat16)
    return (attended, hidden)


RB = 256
KC = 2048
SCORE_FACTOR = math.log2(math.e) / math.sqrt(HD)
MESH = pl.DeviceIdType.MESH


def bit_order(bits, parity):
    order = list(range(bits - 1, -1, -1))
    if parity:
        order[-1], order[-2] = order[-2], order[-1]
    return order


def slot_owners(bits, parity):
    order = bit_order(bits, parity)
    return [sum(((s >> i) & 1) << b for i, b in enumerate(order)) for s in range(1 << bits)]


def fused_kernel(
    bits, groups, group_size, rows,
    q_ref, kn_ref, vn_ref, kpos_ref, rinfo_ref, ck_ref, cv_ref, w_ref, res_ref,
    att_ref, hid_ref,
    kbuf, vbuf, wbuf, vt, s_buf, sn_buf, m_buf, qbuf, o32, stat, osend, orecv, srecv, abuf,
    proj, total, hsend, hrecv,
    load_sem, q_s, q_r, o_s, o_r, t_s, t_r, a_s, a_r, h_s, h_r,
):
    n = 1 << bits
    keys = kbuf.shape[0]
    kc_rows = min(KC, keys)
    chunks = keys // kc_rows
    blocks = n * HD // RB
    per = RB // HD
    me = lax.axis_index("seq")
    core = lax.axis_index("head")

    def my_slot(parity):
        out = 0
        for p in (0, 1):
            slot = 0
            for i, b in enumerate(bit_order(bits, p)):
                slot = slot + (me // (1 << b)) % 2 * (1 << i)
            out = out + slot * (parity if p else 1 - parity)
        return out

    def partner(parity, stage):
        powers = [1 << bit_order(bits, p)[stage] for p in (0, 1)]
        power = powers[0] * (1 - parity) + powers[1] * parity
        return me + (1 - 2 * ((me // power) % 2)) * power

    def remote(src, dst, send, recv, parity, stage):
        return pltpu.make_async_remote_copy(
            src_ref=src, dst_ref=dst, send_sem=send, recv_sem=recv,
            device_id=(partner(parity, stage), core), device_id_type=MESH,
        )

    def gather_copy(buf, send, recv, g, stage):
        parity = g % 2
        size = 1 << stage
        base = my_slot(parity) // size * size
        part = buf.at[g, pl.ds(base, size)]
        return remote(part, part, send.at[g, stage], recv.at[g, stage], parity, stage)

    def gather_step(buf, send, recv, g, stage):
        if stage > 0:
            gather_copy(buf, send, recv, g, stage - 1).wait_recv()
        if stage < bits:
            gather_copy(buf, send, recv, g, stage).start()

    def q_step(g, stage):
        gather_step(qbuf, q_s, q_r, g, stage)

    def a_step(g, stage):
        gather_step(abuf, a_s, a_r, g, stage)

    def reduce_copies(g, stage):
        parity = g % 2
        size = 1 << stage
        slot = my_slot(parity)
        other = slot // size * size + (1 - 2 * ((slot // size) % 2)) * size
        away, land = pl.ds(other, size), pl.ds(size, size)
        return (
            remote(osend.at[g, away], orecv.at[g, land], o_s.at[g, stage], o_r.at[g, stage], parity, stage),
            remote(stat.at[g, away], srecv.at[g, land], t_s.at[g, stage], t_r.at[g, stage], parity, stage),
        )

    def reduce_start(g, stage):
        for copy in reduce_copies(g, stage):
            copy.start()

    def reduce_merge(g, stage):
        for copy in reduce_copies(g, stage):
            copy.wait_recv()
        size = 1 << stage
        kept = my_slot(g % 2) // size * size

        def one(i, unused):
            mine, theirs = stat[g, kept + i], srecv[g, size + i]
            peak = jnp.maximum(mine[0:1], theirs[0:1])
            w_mine, w_theirs = jnp.exp2(mine[0:1] - peak), jnp.exp2(theirs[0:1] - peak)
            sums = mine[1:2] * w_mine + theirs[1:2] * w_theirs
            out = o32[g, kept + i] * w_mine + orecv[g, size + i].astype(jnp.float32) * w_theirs
            o32[g, kept + i] = out
            osend[g, kept + i] = out.astype(jnp.bfloat16)
            stat[g, kept + i] = jnp.concatenate(
                [peak, sums, jnp.zeros((6, HD), jnp.float32)], axis=0
            )
            return 0

        lax.fori_loop(0, size, one, 0)

    def finish(g):
        slot = my_slot(g % 2)
        tile = (o32[g, slot] / stat[g, slot][1:2]).T.astype(jnp.bfloat16)
        for h in range(group_size):
            abuf[g, slot, :, h * HD : (h + 1) * HD] = tile[h * rows : (h + 1) * rows]

    def reduce_step(g, stage):
        reduce_merge(g, stage)
        if stage > 0:
            reduce_start(g, stage - 1)
        else:
            finish(g)
            a_step(g, 0)

    load_v = pltpu.make_async_copy(cv_ref, vbuf, load_sem.at[0])
    load_k = pltpu.make_async_copy(ck_ref, kbuf, load_sem.at[1])
    load_w = pltpu.make_async_copy(w_ref, wbuf, load_sem.at[2])
    load_v.start()
    load_k.start()
    load_w.start()
    barrier = pltpu.get_barrier_semaphore()
    for b in range(bits):
        near = me + (1 - 2 * ((me // (1 << b)) % 2)) * (1 << b)
        pl.semaphore_signal(barrier, inc=1, device_id=(near, core), device_id_type=MESH)
    pl.semaphore_signal(barrier, inc=1, device_id=(me, 1 - core), device_id_type=MESH)
    pl.semaphore_wait(barrier, bits + 1)

    for g in range(groups):
        qbuf[g, my_slot(g % 2)] = q_ref[g]
        q_step(g, 0)

    load_v.wait()

    def transpose_values(g):
        def one(i, unused):
            at = pl.ds(pl.multiple_of(i * 512, 512), 512)
            vt[g, 0:HD, at] = vbuf[at, g * HD : (g + 1) * HD].T
            return 0

        lax.fori_loop(0, keys // 512, one, 0)
        vt[g, 0:HD, keys : keys + HD] = vn_ref[:, g * HD : (g + 1) * HD].T
        vt[g, HD : HD + 16, :] = jnp.ones((16, keys + HD), jnp.bfloat16)

    for g in range(groups):
        transpose_values(g)
        q_step(0, g + 1)
    load_k.wait()

    nt = (((1,), (1,)), ((), ()))

    def query_block(g, rb):
        return qbuf[g, pl.ds(rb * per, per)].reshape(RB, HD)

    def head_lanes(g):
        return pl.ds(pl.multiple_of(g * HD, HD), HD)

    def new_scores(g, rb, slot):
        scores = lax.dot_general(
            kn_ref[:, head_lanes(g)], query_block(g, rb), nt, preferred_element_type=jnp.float32
        )
        cols = pl.ds(pl.multiple_of(rb * RB, RB), RB)
        last, first = rinfo_ref[g % 2, 0:1, cols], rinfo_ref[g % 2, 1:2, cols]
        kpos = kpos_ref[...]
        scores = jnp.where((kpos <= last) & (kpos >= first), scores, -1e30)
        sn_buf[slot] = scores
        return jnp.max(scores.reshape(rows // 8, 8, RB), axis=0)

    def cache_scores(g, rb, kc, slot):
        at = pl.ds(pl.multiple_of(kc * kc_rows, kc_rows), kc_rows)
        scores = lax.dot_general(
            kbuf[at, head_lanes(g)], query_block(g, rb), nt, preferred_element_type=jnp.float32
        )
        s_buf[slot, at, :] = scores
        return jnp.max(scores.reshape(kc_rows // 8, 8, RB), axis=0)

    m_buf[...] = lax.fori_loop(
        0, chunks, lambda kc, m: jnp.maximum(m, cache_scores(0, 0, kc, 0)), new_scores(0, 0, 0)
    )
    steps = groups * blocks

    def step(t, unused):
        g, rb = t // blocks, t % blocks
        for i, stage in ((0, 1), (1, 2), (3, 3), (7, 4)):
            pl.when((rb == i) & (g < groups - 1))(functools.partial(q_step, g + 1, stage))
        pl.when((rb == 0) & (g > 0))(functools.partial(reduce_start, g - 1, bits - 1))
        for i, stage in ((3, 3), (5, 2), (6, 1), (7, 0)):
            pl.when((rb == i) & (g > 0))(functools.partial(reduce_step, g - 1, stage))
        for i, stage in ((0, 1), (1, 2), (3, 3), (6, 4)):
            pl.when((rb == i) & (g > 1))(functools.partial(a_step, g - 2, stage))

        now, later = t % 2, (t + 1) % 2
        after = jnp.minimum(t + 1, steps - 1)
        g2, rb2 = after // blocks, after % blocks
        peak = jnp.max(m_buf[...], axis=0, keepdims=True) * SCORE_FACTOR
        m0 = new_scores(g2, rb2, later)
        p_new = jnp.exp2(sn_buf[now] * SCORE_FACTOR - peak).astype(jnp.bfloat16)
        p_new = jnp.concatenate([p_new, jnp.zeros((HD - rows, RB), jnp.bfloat16)], axis=0)
        acc = jnp.dot(vt[g, :, keys : keys + HD], p_new, preferred_element_type=jnp.float32)

        def inner(kc, carry):
            m, acc = carry
            at = pl.ds(pl.multiple_of(kc * kc_rows, kc_rows), kc_rows)
            p = jnp.exp2(s_buf[now, at, :] * SCORE_FACTOR - peak).astype(jnp.bfloat16)
            acc = acc + jnp.dot(vt[g, :, at], p, preferred_element_type=jnp.float32)
            return jnp.maximum(m, cache_scores(g2, rb2, kc, later)), acc

        m, acc = lax.fori_loop(0, chunks, inner, (m0, acc))
        m_buf[...] = m
        for i in range(per):
            lanes = slice(i * HD, (i + 1) * HD)
            out = acc[0:HD, lanes]
            o32[g, rb * per + i] = out
            osend[g, rb * per + i] = out.astype(jnp.bfloat16)
            stat[g, rb * per + i] = jnp.concatenate(
                [peak[:, lanes], acc[HD : HD + 1, lanes], jnp.zeros((6, HD), jnp.float32)], axis=0
            )
        return 0

    lax.fori_loop(0, steps, step, 0)

    def project(g):
        part = jnp.dot(
            abuf[g].reshape(n * rows, group_size * HD),
            wbuf[g * group_size * HD : (g + 1) * group_size * HD, :],
            preferred_element_type=jnp.float32,
        )
        proj[g % 2] = part if g < 2 else proj[g % 2] + part

    last = groups - 1
    reduce_start(last, bits - 1)
    a_step(last - 1, 1)
    load_w.wait()
    for g in range(last - 1):
        project(g)
    a_step(last - 1, 2)
    a_step(last - 1, 3)
    reduce_step(last, 3)
    reduce_step(last, 2)
    reduce_step(last, 1)
    reduce_step(last, 0)
    a_step(last - 1, 4)
    a_step(last, 1)
    project(last - 1)
    for g in range(groups):
        att_ref[:, g * group_size * HD : (g + 1) * group_size * HD] = abuf[g, my_slot(g % 2)]
    a_step(last, 2)
    a_step(last, 3)
    a_step(last, 4)
    project(last)
    even, odd = slot_owners(bits, 0), slot_owners(bits, 1)
    for owner in range(n):
        se, so = even.index(owner), odd.index(owner)
        tile = proj[0, se * rows : (se + 1) * rows] + proj[1, so * rows : (so + 1) * rows]
        half, at = owner // (n // 2), owner % (n // 2) * rows
        total[half, at : at + rows] = tile
        hsend[half, at : at + rows] = tile.astype(jnp.bfloat16)
    swap = pltpu.make_async_remote_copy(
        src_ref=hsend.at[1 - core], dst_ref=hrecv, send_sem=h_s, recv_sem=h_r,
        device_id=(me, 1 - core), device_id_type=MESH,
    )
    swap.start()
    swap.wait_recv()
    summed = total[core] + hrecv[...].astype(jnp.float32)
    hid_ref[...] = (res_ref[...].astype(jnp.float32) + summed).astype(jnp.bfloat16)
    swap.wait_send()

    def drain(g, unused):
        for stage in range(bits):
            gather_copy(qbuf, q_s, q_r, g, stage).wait_send()
            gather_copy(abuf, a_s, a_r, g, stage).wait_send()
            for copy in reduce_copies(g, stage):
                copy.wait_send()
        return 0

    lax.fori_loop(0, groups, drain, 0)


def fused_device(
    n, queries, cache_keys, cache_values, new_keys, new_values, new_pos, residual, out_weight
):
    bits = n.bit_length() - 1
    rows = queries.shape[0]
    keys = cache_keys.shape[0]
    groups = cache_keys.shape[1] // HD
    group_size = queries.shape[1] // cache_keys.shape[1]
    row_start = lax.axis_index("seq") * rows
    own_pos = lax.dynamic_slice_in_dim(new_pos, row_start, rows)
    own_offsets = own_pos % TURN
    q_rot = rotate(
        queries.astype(jnp.float32).reshape(rows, groups * group_size, HD), own_offsets
    ).astype(jnp.bfloat16)
    q_rot = (
        q_rot.reshape(rows, groups, group_size, HD)
        .transpose(1, 2, 0, 3)
        .reshape(groups, group_size * rows, HD)
    )
    k_rot = rotate(
        new_keys.astype(jnp.float32).reshape(rows, groups, HD), own_offsets
    ).astype(jnp.bfloat16).reshape(rows, groups * HD)
    v_new = jnp.pad(new_values, ((0, HD - rows), (0, 0)))
    kpos = jnp.broadcast_to(own_pos[:, None], (rows, RB))
    infos = []
    for parity in (0, 1):
        table = new_pos.reshape(n, rows)[jnp.array(slot_owners(bits, parity), jnp.int32)]
        table = jnp.broadcast_to(table[:, None, :], (n, group_size, rows)).reshape(-1)
        infos.append(jnp.stack([table, table // TURN * TURN]))
    rinfo = jnp.stack(infos)
    bf, f32 = jnp.bfloat16, jnp.float32
    vmem, hbm = pl.BlockSpec(memory_space=pltpu.VMEM), pl.BlockSpec(memory_space=pl.ANY)
    sems = pltpu.SemaphoreType.DMA((groups, bits))
    width = out_weight.shape[1]
    half = n * rows // 2
    return pl.pallas_call(
        functools.partial(fused_kernel, bits, groups, group_size, rows),
        out_shape=(
            jax.ShapeDtypeStruct(queries.shape, bf),
            jax.ShapeDtypeStruct(residual.shape, bf),
        ),
        in_specs=[vmem] * 5 + [hbm] * 3 + [vmem],
        out_specs=(vmem, vmem),
        scratch_shapes=[
            pltpu.VMEM(cache_keys.shape, bf),
            pltpu.VMEM(cache_values.shape, bf),
            pltpu.VMEM(out_weight.shape, bf),
            pltpu.VMEM((groups, HD + 16, keys + HD), bf),
            pltpu.VMEM((2, keys, RB), f32),
            pltpu.VMEM((2, rows, RB), f32),
            pltpu.VMEM((8, RB), f32),
            pltpu.VMEM((groups, n, HD, HD), bf),
            pltpu.VMEM((groups, n, HD, HD), f32),
            pltpu.VMEM((groups, n, 8, HD), f32),
            pltpu.VMEM((groups, n, HD, HD), bf),
            pltpu.VMEM((groups, n, HD, HD), bf),
            pltpu.VMEM((groups, n, 8, HD), f32),
            pltpu.VMEM((groups, n, rows, group_size * HD), bf),
            pltpu.VMEM((2, n * rows, width), f32),
            pltpu.VMEM((2, half, width), f32),
            pltpu.VMEM((2, half, width), bf),
            pltpu.VMEM((half, width), bf),
            pltpu.SemaphoreType.DMA((3,)),
            sems, sems, sems, sems, sems, sems, sems, sems,
            pltpu.SemaphoreType.DMA,
            pltpu.SemaphoreType.DMA,
        ],
        compiler_params=pltpu.CompilerParams(
            collective_id=0, has_side_effects=True, vmem_limit_bytes=60 * 2**20
        ),
    )(q_rot, k_rot, v_new, kpos, rinfo, cache_keys, cache_values, out_weight, residual)


def on_device(n, *arrays):
    queries, cache_keys = arrays[0], arrays[1]
    rows, keys = queries.shape[0], cache_keys.shape[0]
    groups = cache_keys.shape[1] // HD
    group_size = queries.shape[1] // cache_keys.shape[1]
    fits = n == 16 and groups == 4 and rows == 32 and group_size * rows == HD and keys % KC == 0
    if fits and keys == 4096:
        return fused_device(n, *arrays)
    return plain_device(*arrays)


def solution(mesh):
    return jax.shard_map(
        functools.partial(on_device, mesh.shape["seq"]),
        mesh=mesh,
        in_specs=(
            P("seq", "head"),
            P("seq", "head"),
            P("seq", "head"),
            P("seq", "head"),
            P("seq", "head"),
            P(),
            P("head", "seq"),
            P("head", "seq"),
        ),
        out_specs=(P("seq", "head"), P("head", "seq")),
        check_vma=False,
    )
```

```python
import functools
import math

import jax
import jax.numpy as jnp
from jax import lax
from jax.experimental import pallas as pl
from jax.experimental.pallas import tpu as pltpu
from jax.sharding import PartitionSpec as P

HD = 128
TURN = 128


rope_base = 3580165449.0


def rotate(vectors, offsets):
    half_width = vectors.shape[-1] // 2
    frequency = jnp.exp(
        jnp.arange(half_width, dtype=jnp.float32) * (-2.0 * math.log(rope_base) / vectors.shape[-1])
    )
    angles = offsets.astype(jnp.float32)[:, None] * frequency[None, :]
    cosine = jnp.concatenate([jnp.cos(angles), jnp.cos(angles)], axis=-1)[:, None, :]
    sine_part = jnp.concatenate([jnp.sin(angles), jnp.sin(angles)], axis=-1)[:, None, :]
    turned = jnp.concatenate([-vectors[..., half_width:], vectors[..., :half_width]], axis=-1)
    return vectors * cosine + turned * sine_part


def fold_scores(carry, scores, value_block, visible):
    running_max, running_sum, running_out = carry
    new_max = jnp.maximum(running_max, jnp.max(scores, axis=-1))
    shrink = jnp.exp(running_max - new_max)
    exps = jnp.exp(scores - new_max[..., None])
    if visible is not None:
        exps = jnp.where(visible, exps, 0.0)
    running_sum = running_sum * shrink + jnp.sum(exps, axis=-1)
    product = jnp.einsum(
        "grk,kgd->grd", exps.astype(jnp.bfloat16), value_block, preferred_element_type=jnp.float32
    )
    running_out = running_out * shrink[..., None] + product
    return (new_max, running_sum, running_out)


def plain_device(
    queries, cache_keys, cache_values, new_keys, new_values, new_pos, residual, out_weight
):
    local_rows = queries.shape[0]
    kv_local = cache_keys.shape[1] // HD
    group_size = queries.shape[1] // cache_keys.shape[1]
    offsets = new_pos % TURN
    turn_ids = new_pos // TURN
    row_start = lax.axis_index("seq") * local_rows
    own_offsets = lax.dynamic_slice_in_dim(offsets, row_start, local_rows)
    own_turns = lax.dynamic_slice_in_dim(turn_ids, row_start, local_rows)
    query_rot = rotate(
        queries.astype(jnp.float32).reshape(local_rows, kv_local * group_size, HD), own_offsets
    )
    query_rot = query_rot.astype(jnp.bfloat16).reshape(local_rows, kv_local * group_size * HD)
    key_rot = rotate(
        new_keys.astype(jnp.float32).reshape(local_rows, kv_local, HD), own_offsets
    ).astype(jnp.bfloat16)
    all_queries = lax.all_gather(query_rot, "seq", axis=0, tiled=True)
    total_rows = all_queries.shape[0]
    head_local = kv_local * group_size
    grouped = (
        all_queries.reshape(total_rows, kv_local, group_size, HD)
        .transpose(1, 0, 2, 3)
        .reshape(kv_local, total_rows * group_size, HD)
    )
    score_scale = 1.0 / math.sqrt(HD)
    block_rows = min(512, cache_keys.shape[0])
    block_count = cache_keys.shape[0] // block_rows
    key_blocks = cache_keys.reshape(block_count, block_rows, kv_local, HD)
    value_blocks = cache_values.reshape(block_count, block_rows, kv_local, HD)

    def absorb(carry, blocks):
        scores = (
            jnp.einsum("grd,kgd->grk", grouped, blocks[0], preferred_element_type=jnp.float32)
            * score_scale
        )
        return (fold_scores(carry, scores, blocks[1], None), None)

    start_max = jnp.full((kv_local, total_rows * group_size), -1e30, jnp.float32)
    start_sum = jnp.zeros((kv_local, total_rows * group_size), jnp.float32)
    start_out = jnp.zeros((kv_local, total_rows * group_size, HD), jnp.float32)
    carry, unused = lax.scan(absorb, (start_max, start_sum, start_out), (key_blocks, value_blocks))
    visible = (turn_ids[:, None] == own_turns[None, :]) & (own_offsets[None, :] <= offsets[:, None])
    visible = jnp.repeat(visible, group_size, axis=0)[None]
    scores = (
        jnp.einsum("grd,kgd->grk", grouped, key_rot, preferred_element_type=jnp.float32)
        * score_scale
    )
    masked = jnp.where(visible, scores, -1e30)
    value_new = new_values.reshape(local_rows, kv_local, HD)
    running_max, running_sum, running_out = fold_scores(carry, masked, value_new, visible)
    out_rows = (
        running_out.reshape(kv_local, total_rows, group_size, HD)
        .transpose(1, 0, 2, 3)
        .reshape(total_rows, head_local * HD)
    )
    max_rows = (
        running_max.reshape(kv_local, total_rows, group_size)
        .transpose(1, 0, 2)
        .reshape(total_rows, head_local)
    )
    sum_rows = (
        running_sum.reshape(kv_local, total_rows, group_size)
        .transpose(1, 0, 2)
        .reshape(total_rows, head_local)
    )
    partials, maxima, totals = (
        lax.all_to_all(out_rows[None], "seq", split_axis=1, concat_axis=0, tiled=True),
        lax.all_to_all(max_rows[None], "seq", split_axis=1, concat_axis=0, tiled=True),
        lax.all_to_all(sum_rows[None], "seq", split_axis=1, concat_axis=0, tiled=True),
    )
    peak_score = jnp.max(maxima, axis=0)
    weight = jnp.exp(maxima - peak_score[None])
    numerator = jnp.sum(
        partials.reshape(partials.shape[0], local_rows, head_local, HD) * weight[..., None], axis=0
    )
    denominator = jnp.sum(totals * weight, axis=0)
    attended = (
        (numerator / denominator[..., None])
        .reshape(local_rows, head_local * HD)
        .astype(jnp.bfloat16)
    )
    projected = jnp.dot(
        lax.all_gather(attended, "seq", axis=0, tiled=True),
        out_weight,
        preferred_element_type=jnp.float32,
    )
    summed = lax.psum_scatter(
        projected.astype(jnp.bfloat16), "head", scatter_dimension=0, tiled=True
    ).astype(jnp.float32)
    hidden = (residual.astype(jnp.float32) + summed).astype(jnp.bfloat16)
    return (attended, hidden)


RB = 256
KC = 2048
SCORE_FACTOR = math.log2(math.e) / math.sqrt(HD)
MESH = pl.DeviceIdType.MESH


def bit_order(bits, parity):
    order = list(range(bits - 1, -1, -1))
    if parity:
        order[-1], order[-2] = order[-2], order[-1]
    return order


def slot_owners(bits, parity):
    order = bit_order(bits, parity)
    return [sum(((s >> i) & 1) << b for i, b in enumerate(order)) for s in range(1 << bits)]


def fused_kernel(
    bits, groups, group_size, rows,
    q_ref, kn_ref, vn_ref, trig_ref, kpos_ref, rinfo_ref, ck_ref, cv_ref, w_ref, res_ref,
    att_ref, hid_ref,
    kbuf, vbuf, wbuf, vt, s_buf, sn_buf, m_buf, qbuf, o32, stat, osend, orecv, srecv, abuf,
    proj, total, hsend, hrecv,
    knew, load_sem, q_s, q_r, o_s, o_r, t_s, t_r, a_s, a_r, h_s, h_r, d_s, d_r,
):
    n = 1 << bits
    keys = kbuf.shape[0]
    kc_rows = min(KC, keys)
    chunks = keys // kc_rows
    blocks = n * HD // RB
    per = RB // HD
    me = lax.axis_index("seq")
    core = lax.axis_index("head")

    def my_slot(parity):
        out = 0
        for p in (0, 1):
            slot = 0
            for i, b in enumerate(bit_order(bits, p)):
                slot = slot + (me // (1 << b)) % 2 * (1 << i)
            out = out + slot * (parity if p else 1 - parity)
        return out

    def partner(parity, stage):
        powers = [1 << bit_order(bits, p)[stage] for p in (0, 1)]
        power = powers[0] * (1 - parity) + powers[1] * parity
        return me + (1 - 2 * ((me // power) % 2)) * power

    def remote(src, dst, send, recv, parity, stage):
        return pltpu.make_async_remote_copy(
            src_ref=src, dst_ref=dst, send_sem=send, recv_sem=recv,
            device_id=(partner(parity, stage), core), device_id_type=MESH,
        )

    def gather_copy(buf, send, recv, g, stage):
        parity = g % 2
        size = 1 << stage
        base = my_slot(parity) // size * size
        part = buf.at[g, pl.ds(base, size)]
        return remote(part, part, send.at[g, stage], recv.at[g, stage], parity, stage)

    def gather_step(buf, send, recv, g, stage):
        if stage > 0:
            gather_copy(buf, send, recv, g, stage - 1).wait_recv()
        if stage < bits:
            gather_copy(buf, send, recv, g, stage).start()

    def q_step(g, stage):
        gather_step(qbuf, q_s, q_r, g, stage)

    def a_step(g, stage):
        gather_step(abuf, a_s, a_r, g, stage)

    def reduce_copies(g, stage):
        parity = g % 2
        size = 1 << stage
        slot = my_slot(parity)
        other = slot // size * size + (1 - 2 * ((slot // size) % 2)) * size
        away, land = pl.ds(other, size), pl.ds(size, size)
        return (
            remote(osend.at[g, away], orecv.at[g, land], o_s.at[g, stage], o_r.at[g, stage], parity, stage),
            remote(stat.at[g, away], srecv.at[g, land], t_s.at[g, stage], t_r.at[g, stage], parity, stage),
        )

    def reduce_start(g, stage):
        for copy in reduce_copies(g, stage):
            copy.start()

    def reduce_merge(g, stage):
        for copy in reduce_copies(g, stage):
            copy.wait_recv()
        size = 1 << stage
        kept = my_slot(g % 2) // size * size

        def one(i, unused):
            mine, theirs = stat[g, kept + i], srecv[g, size + i]
            peak = jnp.maximum(mine[0:1], theirs[0:1])
            w_mine, w_theirs = jnp.exp2(mine[0:1] - peak), jnp.exp2(theirs[0:1] - peak)
            sums = mine[1:2] * w_mine + theirs[1:2] * w_theirs
            out = o32[g, kept + i] * w_mine + orecv[g, size + i].astype(jnp.float32) * w_theirs
            o32[g, kept + i] = out
            osend[g, kept + i] = out.astype(jnp.bfloat16)
            stat[g, kept + i] = jnp.concatenate(
                [peak, sums, jnp.zeros((6, HD), jnp.float32)], axis=0
            )
            return 0

        lax.fori_loop(0, size, one, 0)

    def finish(g):
        slot = my_slot(g % 2)
        tile = (o32[g, slot] / stat[g, slot][1:2]).T.astype(jnp.bfloat16)
        for h in range(group_size):
            abuf[g, slot, :, h * HD : (h + 1) * HD] = tile[h * rows : (h + 1) * rows]

    def reduce_step(g, stage):
        reduce_merge(g, stage)
        if stage > 0:
            reduce_start(g, stage - 1)
        else:
            finish(g)
            a_step(g, 0)

    def flip(mask):
        out = me
        for b in range(bits):
            if mask >> b & 1:
                out = out + (1 - 2 * ((me // (1 << b)) % 2)) * (1 << b)
        return out

    def flip_slot(slot, delta):
        for b in range(bits):
            if delta >> b & 1:
                slot = slot + (1 - 2 * ((slot // (1 << b)) % 2)) * (1 << b)
        return slot

    def device_at(g, delta):
        order = bit_order(bits, g % 2)
        return flip(sum(1 << order[b] for b in range(bits) if delta >> b & 1))

    def direct(src, dst, kind, g, delta, i):
        return pltpu.make_async_remote_copy(
            src_ref=src, dst_ref=dst, send_sem=d_s.at[kind, i], recv_sem=d_r.at[kind, i],
            device_id=(device_at(g, delta), core), device_id_type=MESH,
        )

    def spread_copies(g, phase):
        size = 1 if phase == 0 else 4
        part = abuf.at[g, pl.ds(my_slot(g % 2) // size * size, size)]
        return [direct(part, part, phase, g, i * size, i - 1) for i in (1, 2, 3)]

    def last_copies(g):
        out = []
        slot = my_slot(g % 2)
        for i in (1, 2, 3):
            away = flip_slot(slot, i)
            out.append(direct(osend.at[g, away], orecv.at[g, i], 2, g, i, i - 1))
            out.append(direct(stat.at[g, away], srecv.at[g, i], 3, g, i, i - 1))
        return out

    def last_merge(g):
        slot = my_slot(g % 2)
        stats = [stat[g, slot]] + [srecv[g, i] for i in (1, 2, 3)]
        peak = functools.reduce(jnp.maximum, [x[0:1] for x in stats])
        weights = [jnp.exp2(x[0:1] - peak) for x in stats]
        outs = [o32[g, slot]] + [orecv[g, i].astype(jnp.float32) for i in (1, 2, 3)]
        sums = sum(x[1:2] * w for x, w in zip(stats, weights))
        o32[g, slot] = sum(o * w for o, w in zip(outs, weights))
        stat[g, slot] = jnp.concatenate([peak, sums, jnp.zeros((6, HD), jnp.float32)], axis=0)

    load_v = pltpu.make_async_copy(cv_ref, vbuf, load_sem.at[0])
    load_k = pltpu.make_async_copy(ck_ref, kbuf, load_sem.at[1])
    load_w = pltpu.make_async_copy(w_ref, wbuf, load_sem.at[2])
    load_v.start()
    load_k.start()
    load_w.start()
    barrier = pltpu.get_barrier_semaphore()
    masks = [1 << b for b in range(bits)] + [3, 3 << (bits - 2)]
    for mask in masks:
        pl.semaphore_signal(barrier, inc=1, device_id=(flip(mask), core), device_id_type=MESH)
    pl.semaphore_signal(barrier, inc=1, device_id=(me, 1 - core), device_id_type=MESH)

    def barrier_wait():
        pl.semaphore_wait(barrier, len(masks) + 1)

    cosine, sine = trig_ref[0], trig_ref[1]

    def turned(block):
        x = block.astype(jnp.float32)
        return (x * cosine + pltpu.roll(x, HD // 2, 1) * sine).astype(jnp.bfloat16)

    for g in range(groups):
        slot = my_slot(g % 2)
        for h in range(group_size):
            at = (g * group_size + h) * HD
            qbuf[g, slot, h * rows : (h + 1) * rows] = turned(q_ref[:, at : at + HD])
    barrier_wait()
    for g in range(groups):
        q_step(g, 0)
    for g in range(groups):
        knew[:, g * HD : (g + 1) * HD] = turned(kn_ref[:, g * HD : (g + 1) * HD])

    load_v.wait()

    def transpose_values(g):
        def one(i, unused):
            at = pl.ds(pl.multiple_of(i * 512, 512), 512)
            vt[g, 0:HD, at] = vbuf[at, g * HD : (g + 1) * HD].T
            return 0

        lax.fori_loop(0, keys // 512, one, 0)
        fresh = jnp.concatenate(
            [vn_ref[:, g * HD : (g + 1) * HD], jnp.zeros((HD - rows, HD), jnp.bfloat16)], axis=0
        )
        vt[g, 0:HD, keys : keys + HD] = fresh.T
        vt[g, HD : HD + 16, :] = jnp.ones((16, keys + HD), jnp.bfloat16)

    transpose_values(0)
    q_step(0, 1)
    for g in range(1, groups):
        transpose_values(g)
    load_k.wait()

    nt = (((1,), (1,)), ((), ()))

    def query_block(g, rb):
        return qbuf[g, pl.ds(rb * per, per)].reshape(RB, HD)

    def head_lanes(g):
        return pl.ds(pl.multiple_of(g * HD, HD), HD)

    def new_scores(g, rb, slot):
        scores = lax.dot_general(
            knew[:, head_lanes(g)], query_block(g, rb), nt, preferred_element_type=jnp.float32
        )
        cols = pl.ds(pl.multiple_of(rb * RB, RB), RB)
        last = rinfo_ref[g % 2, :, cols]
        first = last - (last & (TURN - 1))
        kpos = kpos_ref[...]
        scores = jnp.where((kpos <= last) & (kpos >= first), scores, -1e30)
        sn_buf[slot] = scores
        return jnp.max(scores.reshape(rows // 8, 8, RB), axis=0)

    def cache_scores(g, rb, kc, slot):
        at = pl.ds(pl.multiple_of(kc * kc_rows, kc_rows), kc_rows)
        scores = lax.dot_general(
            kbuf[at, head_lanes(g)], query_block(g, rb), nt, preferred_element_type=jnp.float32
        )
        s_buf[slot, at, :] = scores
        return jnp.max(scores.reshape(kc_rows // 8, 8, RB), axis=0)

    levels = blocks.bit_length() - 1

    def block_at(g, j):
        first = 1 - jnp.minimum(g, 1)
        mine = my_slot(g % 2) // per
        out = 0
        for b in range(levels):
            same = (mine // (1 << b) + j // (1 << b) + 1 - first) % 2
            out = out + same * (1 << b)
        return out

    start = block_at(0, 0)
    m_buf[...] = lax.fori_loop(
        0, chunks, lambda kc, m: jnp.maximum(m, cache_scores(0, start, kc, 0)),
        new_scores(0, start, 0),
    )
    steps = groups * blocks

    def step(t, unused):
        g, j = t // blocks, t % blocks
        for i, stage in ((0, 2), (1, 3), (3, 4)):
            pl.when(t == i)(functools.partial(q_step, 0, stage))
        for i, stage in ((0, 1), (1, 2), (3, 3), (7, 4)):
            pl.when((j == i) & (g < groups - 1))(functools.partial(q_step, g + 1, stage))
        pl.when((j == 4) & (g > 0))(functools.partial(reduce_start, g, bits - 1))
        pl.when(t == blocks)(functools.partial(reduce_start, 0, bits - 1))
        for i, stage in ((3, 3), (5, 2), (6, 1), (7, 0)):
            pl.when((j == i) & (g == 1))(functools.partial(reduce_step, 0, stage))
        for i, stage in ((0, 3), (2, 2), (3, 1), (4, 0)):
            pl.when((j == i) & (g > 1))(functools.partial(reduce_step, g - 1, stage))
        for i, stage in ((0, 1), (1, 2), (2, 3), (5, 4)):
            pl.when((j == i) & (g == 2))(functools.partial(a_step, 0, stage))
        for i, stage in ((5, 1), (6, 2), (7, 3)):
            pl.when((j == i) & (g > 1))(functools.partial(a_step, g - 1, stage))
        pl.when((j == 2) & (g > 2))(functools.partial(a_step, g - 2, 4))
        rb = block_at(g, j)

        now, later = t % 2, (t + 1) % 2
        after = jnp.minimum(t + 1, steps - 1)
        g2 = after // blocks
        rb2 = block_at(g2, after % blocks)
        peak = jnp.max(m_buf[...], axis=0, keepdims=True) * SCORE_FACTOR
        m0 = new_scores(g2, rb2, later)
        p_new = jnp.exp2(sn_buf[now] * SCORE_FACTOR - peak).astype(jnp.bfloat16)
        p_new = jnp.concatenate([p_new, jnp.zeros((HD - rows, RB), jnp.bfloat16)], axis=0)
        acc = jnp.dot(vt[g, :, keys : keys + HD], p_new, preferred_element_type=jnp.float32)

        def inner(kc, carry):
            m, acc = carry
            at = pl.ds(pl.multiple_of(kc * kc_rows, kc_rows), kc_rows)
            p = jnp.exp2(s_buf[now, at, :] * SCORE_FACTOR - peak).astype(jnp.bfloat16)
            acc = acc + jnp.dot(vt[g, :, at], p, preferred_element_type=jnp.float32)
            return jnp.maximum(m, cache_scores(g2, rb2, kc, later)), acc

        m, acc = lax.fori_loop(0, chunks, inner, (m0, acc))
        m_buf[...] = m
        for i in range(per):
            lanes = slice(i * HD, (i + 1) * HD)
            out = acc[0:HD, lanes]
            o32[g, rb * per + i] = out
            osend[g, rb * per + i] = out.astype(jnp.bfloat16)
            stat[g, rb * per + i] = jnp.concatenate(
                [peak[:, lanes], acc[HD : HD + 1, lanes], jnp.zeros((6, HD), jnp.float32)], axis=0
            )
        return 0

    lax.fori_loop(0, steps, step, 0)

    def project(g):
        part = jnp.dot(
            abuf[g].reshape(n * rows, group_size * HD),
            wbuf[g * group_size * HD : (g + 1) * group_size * HD, :],
            preferred_element_type=jnp.float32,
        )
        proj[g % 2] = part if g < 2 else proj[g % 2] + part

    last = groups - 1
    reduce_step(last, 3)
    load_w.wait()
    for g in range(last - 1):
        project(g)
    reduce_merge(last, 2)
    for copy in last_copies(last):
        copy.start()
    a_step(last - 1, 4)
    project(last - 1)
    for copy in last_copies(last):
        copy.wait_recv()
    last_merge(last)
    finish(last)
    for copy in spread_copies(last, 0):
        copy.start()
    for g in range(groups):
        att_ref[:, g * group_size * HD : (g + 1) * group_size * HD] = abuf[g, my_slot(g % 2)]
    for copy in spread_copies(last, 0):
        copy.wait_recv()
    for copy in spread_copies(last, 1):
        copy.start()
    for copy in spread_copies(last, 1):
        copy.wait_recv()
    project(last)
    even, odd = slot_owners(bits, 0), slot_owners(bits, 1)
    for owner in range(n):
        se, so = even.index(owner), odd.index(owner)
        tile = proj[0, se * rows : (se + 1) * rows] + proj[1, so * rows : (so + 1) * rows]
        half, at = owner // (n // 2), owner % (n // 2) * rows
        total[half, at : at + rows] = tile
        hsend[half, at : at + rows] = tile.astype(jnp.bfloat16)
    swap = pltpu.make_async_remote_copy(
        src_ref=hsend.at[1 - core], dst_ref=hrecv, send_sem=h_s, recv_sem=h_r,
        device_id=(me, 1 - core), device_id_type=MESH,
    )
    swap.start()
    swap.wait_recv()
    summed = total[core] + hrecv[...].astype(jnp.float32)
    hid_ref[...] = (res_ref[...].astype(jnp.float32) + summed).astype(jnp.bfloat16)
    swap.wait_send()

    def drain(g, unused):
        for stage in range(bits):
            gather_copy(qbuf, q_s, q_r, g, stage).wait_send()
        for stage in (2, 3):
            for copy in reduce_copies(g, stage):
                copy.wait_send()
        return 0

    def drain_rest(g, unused):
        for stage in range(bits):
            gather_copy(abuf, a_s, a_r, g, stage).wait_send()
        for stage in (0, 1):
            for copy in reduce_copies(g, stage):
                copy.wait_send()
        return 0

    lax.fori_loop(0, groups, drain, 0)
    lax.fori_loop(0, last, drain_rest, 0)
    for copy in last_copies(last) + spread_copies(last, 0) + spread_copies(last, 1):
        copy.wait_send()


def fused_device(
    n, queries, cache_keys, cache_values, new_keys, new_values, new_pos, residual, out_weight
):
    bits = n.bit_length() - 1
    rows = queries.shape[0]
    keys = cache_keys.shape[0]
    groups = cache_keys.shape[1] // HD
    group_size = queries.shape[1] // cache_keys.shape[1]
    row_start = lax.axis_index("seq") * rows
    own_pos = lax.dynamic_slice_in_dim(new_pos, row_start, rows)
    frequency = jnp.exp(
        (jnp.arange(HD, dtype=jnp.int32) % (HD // 2)).astype(jnp.float32)
        * (-2.0 * math.log(rope_base) / HD)
    )
    angles = (own_pos % TURN).astype(jnp.float32)[:, None] * frequency[None, :]
    sign = jnp.where(jnp.arange(HD) < HD // 2, -1.0, 1.0)
    trig = jnp.stack([jnp.cos(angles), jnp.sin(angles) * sign])
    kpos = jnp.broadcast_to(own_pos[:, None], (rows, RB))
    infos = []
    for parity in (0, 1):
        axes = [bits - 1 - b for b in reversed(bit_order(bits, parity))]
        table = new_pos.reshape((2,) * bits + (rows,)).transpose(*axes, bits).reshape(n, 1, rows)
        infos.append(jnp.broadcast_to(table, (n, group_size, rows)).reshape(1, -1))
    rinfo = jnp.stack(infos)
    bf, f32 = jnp.bfloat16, jnp.float32
    vmem, hbm = pl.BlockSpec(memory_space=pltpu.VMEM), pl.BlockSpec(memory_space=pl.ANY)
    sems = pltpu.SemaphoreType.DMA((groups, bits))
    width = out_weight.shape[1]
    half = n * rows // 2
    return pl.pallas_call(
        functools.partial(fused_kernel, bits, groups, group_size, rows),
        out_shape=(
            jax.ShapeDtypeStruct(queries.shape, bf),
            jax.ShapeDtypeStruct(residual.shape, bf),
        ),
        in_specs=[vmem] * 6 + [hbm] * 3 + [vmem],
        out_specs=(vmem, vmem),
        scratch_shapes=[
            pltpu.VMEM(cache_keys.shape, bf),
            pltpu.VMEM(cache_values.shape, bf),
            pltpu.VMEM(out_weight.shape, bf),
            pltpu.VMEM((groups, HD + 16, keys + HD), bf),
            pltpu.VMEM((2, keys, RB), f32),
            pltpu.VMEM((2, rows, RB), f32),
            pltpu.VMEM((8, RB), f32),
            pltpu.VMEM((groups, n, HD, HD), bf),
            pltpu.VMEM((groups, n, HD, HD), f32),
            pltpu.VMEM((groups, n, 8, HD), f32),
            pltpu.VMEM((groups, n, HD, HD), bf),
            pltpu.VMEM((groups, n, HD, HD), bf),
            pltpu.VMEM((groups, n, 8, HD), f32),
            pltpu.VMEM((groups, n, rows, group_size * HD), bf),
            pltpu.VMEM((2, n * rows, width), f32),
            pltpu.VMEM((2, half, width), f32),
            pltpu.VMEM((2, half, width), bf),
            pltpu.VMEM((half, width), bf),
            pltpu.VMEM(new_keys.shape, bf),
            pltpu.SemaphoreType.DMA((3,)),
            sems, sems, sems, sems, sems, sems, sems, sems,
            pltpu.SemaphoreType.DMA,
            pltpu.SemaphoreType.DMA,
            pltpu.SemaphoreType.DMA((4, 3)),
            pltpu.SemaphoreType.DMA((4, 3)),
        ],
        compiler_params=pltpu.CompilerParams(
            collective_id=0, has_side_effects=True, vmem_limit_bytes=60 * 2**20
        ),
    )(
        queries, new_keys, new_values, trig, kpos, rinfo,
        cache_keys, cache_values, out_weight, residual,
    )


def on_device(n, *arrays):
    queries, cache_keys = arrays[0], arrays[1]
    rows, keys = queries.shape[0], cache_keys.shape[0]
    groups = cache_keys.shape[1] // HD
    group_size = queries.shape[1] // cache_keys.shape[1]
    fits = n == 16 and groups == 4 and rows == 32 and group_size * rows == HD and keys % KC == 0
    if fits and keys == 4096:
        return fused_device(n, *arrays)
    return plain_device(*arrays)


def solution(mesh):
    return jax.shard_map(
        functools.partial(on_device, mesh.shape["seq"]),
        mesh=mesh,
        in_specs=(
            P("seq", "head"),
            P("seq", "head"),
            P("seq", "head"),
            P("seq", "head"),
            P("seq", "head"),
            P(),
            P("head", "seq"),
            P("head", "seq"),
        ),
        out_specs=(P("seq", "head"), P("head", "seq")),
        check_vma=False,
    )
```

```python
import functools
import math

import jax
import jax.numpy as jnp
from jax import lax
from jax.experimental import pallas as pl
from jax.experimental.pallas import tpu as pltpu
from jax.sharding import PartitionSpec as P

HD = 128
TURN = 128


rope_base = 3580165449.0


def rotate(vectors, offsets):
    half_width = vectors.shape[-1] // 2
    frequency = jnp.exp(
        jnp.arange(half_width, dtype=jnp.float32) * (-2.0 * math.log(rope_base) / vectors.shape[-1])
    )
    angles = offsets.astype(jnp.float32)[:, None] * frequency[None, :]
    cosine = jnp.concatenate([jnp.cos(angles), jnp.cos(angles)], axis=-1)[:, None, :]
    sine_part = jnp.concatenate([jnp.sin(angles), jnp.sin(angles)], axis=-1)[:, None, :]
    turned = jnp.concatenate([-vectors[..., half_width:], vectors[..., :half_width]], axis=-1)
    return vectors * cosine + turned * sine_part


def fold_scores(carry, scores, value_block, visible):
    running_max, running_sum, running_out = carry
    new_max = jnp.maximum(running_max, jnp.max(scores, axis=-1))
    shrink = jnp.exp(running_max - new_max)
    exps = jnp.exp(scores - new_max[..., None])
    if visible is not None:
        exps = jnp.where(visible, exps, 0.0)
    running_sum = running_sum * shrink + jnp.sum(exps, axis=-1)
    product = jnp.einsum(
        "grk,kgd->grd", exps.astype(jnp.bfloat16), value_block, preferred_element_type=jnp.float32
    )
    running_out = running_out * shrink[..., None] + product
    return (new_max, running_sum, running_out)


def plain_device(
    queries, cache_keys, cache_values, new_keys, new_values, new_pos, residual, out_weight
):
    local_rows = queries.shape[0]
    kv_local = cache_keys.shape[1] // HD
    group_size = queries.shape[1] // cache_keys.shape[1]
    offsets = new_pos % TURN
    turn_ids = new_pos // TURN
    row_start = lax.axis_index("seq") * local_rows
    own_offsets = lax.dynamic_slice_in_dim(offsets, row_start, local_rows)
    own_turns = lax.dynamic_slice_in_dim(turn_ids, row_start, local_rows)
    query_rot = rotate(
        queries.astype(jnp.float32).reshape(local_rows, kv_local * group_size, HD), own_offsets
    )
    query_rot = query_rot.astype(jnp.bfloat16).reshape(local_rows, kv_local * group_size * HD)
    key_rot = rotate(
        new_keys.astype(jnp.float32).reshape(local_rows, kv_local, HD), own_offsets
    ).astype(jnp.bfloat16)
    all_queries = lax.all_gather(query_rot, "seq", axis=0, tiled=True)
    total_rows = all_queries.shape[0]
    head_local = kv_local * group_size
    grouped = (
        all_queries.reshape(total_rows, kv_local, group_size, HD)
        .transpose(1, 0, 2, 3)
        .reshape(kv_local, total_rows * group_size, HD)
    )
    score_scale = 1.0 / math.sqrt(HD)
    block_rows = min(512, cache_keys.shape[0])
    block_count = cache_keys.shape[0] // block_rows
    key_blocks = cache_keys.reshape(block_count, block_rows, kv_local, HD)
    value_blocks = cache_values.reshape(block_count, block_rows, kv_local, HD)

    def absorb(carry, blocks):
        scores = (
            jnp.einsum("grd,kgd->grk", grouped, blocks[0], preferred_element_type=jnp.float32)
            * score_scale
        )
        return (fold_scores(carry, scores, blocks[1], None), None)

    start_max = jnp.full((kv_local, total_rows * group_size), -1e30, jnp.float32)
    start_sum = jnp.zeros((kv_local, total_rows * group_size), jnp.float32)
    start_out = jnp.zeros((kv_local, total_rows * group_size, HD), jnp.float32)
    carry, unused = lax.scan(absorb, (start_max, start_sum, start_out), (key_blocks, value_blocks))
    visible = (turn_ids[:, None] == own_turns[None, :]) & (own_offsets[None, :] <= offsets[:, None])
    visible = jnp.repeat(visible, group_size, axis=0)[None]
    scores = (
        jnp.einsum("grd,kgd->grk", grouped, key_rot, preferred_element_type=jnp.float32)
        * score_scale
    )
    masked = jnp.where(visible, scores, -1e30)
    value_new = new_values.reshape(local_rows, kv_local, HD)
    running_max, running_sum, running_out = fold_scores(carry, masked, value_new, visible)
    out_rows = (
        running_out.reshape(kv_local, total_rows, group_size, HD)
        .transpose(1, 0, 2, 3)
        .reshape(total_rows, head_local * HD)
    )
    max_rows = (
        running_max.reshape(kv_local, total_rows, group_size)
        .transpose(1, 0, 2)
        .reshape(total_rows, head_local)
    )
    sum_rows = (
        running_sum.reshape(kv_local, total_rows, group_size)
        .transpose(1, 0, 2)
        .reshape(total_rows, head_local)
    )
    partials, maxima, totals = (
        lax.all_to_all(out_rows[None], "seq", split_axis=1, concat_axis=0, tiled=True),
        lax.all_to_all(max_rows[None], "seq", split_axis=1, concat_axis=0, tiled=True),
        lax.all_to_all(sum_rows[None], "seq", split_axis=1, concat_axis=0, tiled=True),
    )
    peak_score = jnp.max(maxima, axis=0)
    weight = jnp.exp(maxima - peak_score[None])
    numerator = jnp.sum(
        partials.reshape(partials.shape[0], local_rows, head_local, HD) * weight[..., None], axis=0
    )
    denominator = jnp.sum(totals * weight, axis=0)
    attended = (
        (numerator / denominator[..., None])
        .reshape(local_rows, head_local * HD)
        .astype(jnp.bfloat16)
    )
    projected = jnp.dot(
        lax.all_gather(attended, "seq", axis=0, tiled=True),
        out_weight,
        preferred_element_type=jnp.float32,
    )
    summed = lax.psum_scatter(
        projected.astype(jnp.bfloat16), "head", scatter_dimension=0, tiled=True
    ).astype(jnp.float32)
    hidden = (residual.astype(jnp.float32) + summed).astype(jnp.bfloat16)
    return (attended, hidden)


RB = 256
KC = 2048
SCORE_FACTOR = math.log2(math.e) / math.sqrt(HD)
MESH = pl.DeviceIdType.MESH


def bit_order(bits, parity):
    order = list(range(bits - 1, -1, -1))
    if parity:
        order[-1], order[-2] = order[-2], order[-1]
    return order


def slot_owners(bits, parity):
    order = bit_order(bits, parity)
    return [sum(((s >> i) & 1) << b for i, b in enumerate(order)) for s in range(1 << bits)]


def fused_kernel(
    bits, groups, group_size, rows,
    q_ref, kn_ref, vn_ref, trig_ref, kpos_ref, rinfo_ref, ck_ref, cv_ref, w_ref, res_ref,
    att_ref, hid_ref,
    kbuf, vbuf, wbuf, vt, s_buf, sn_buf, m_buf, qbuf, o32, stat, osend, orecv, srecv, abuf,
    proj, total, hsend, hrecv,
    knew, load_sem, q_s, q_r, o_s, o_r, t_s, t_r, a_s, a_r, h_s, h_r, d_s, d_r,
):
    n = 1 << bits
    keys = kbuf.shape[0]
    kc_rows = min(KC, keys)
    chunks = keys // kc_rows
    blocks = n * HD // RB
    per = RB // HD
    me = lax.axis_index("seq")
    core = lax.axis_index("head")

    def my_slot(parity):
        out = 0
        for p in (0, 1):
            slot = 0
            for i, b in enumerate(bit_order(bits, p)):
                slot = slot + (me // (1 << b)) % 2 * (1 << i)
            out = out + slot * (parity if p else 1 - parity)
        return out

    def partner(parity, stage):
        powers = [1 << bit_order(bits, p)[stage] for p in (0, 1)]
        power = powers[0] * (1 - parity) + powers[1] * parity
        return me + (1 - 2 * ((me // power) % 2)) * power

    def remote(src, dst, send, recv, parity, stage):
        return pltpu.make_async_remote_copy(
            src_ref=src, dst_ref=dst, send_sem=send, recv_sem=recv,
            device_id=(partner(parity, stage), core), device_id_type=MESH,
        )

    def gather_copy(buf, send, recv, g, stage):
        parity = g % 2
        size = 1 << stage
        base = my_slot(parity) // size * size
        part = buf.at[g, pl.ds(base, size)]
        return remote(part, part, send.at[g, stage], recv.at[g, stage], parity, stage)

    def gather_step(buf, send, recv, g, stage):
        if stage > 0:
            gather_copy(buf, send, recv, g, stage - 1).wait_recv()
        if stage < bits:
            gather_copy(buf, send, recv, g, stage).start()

    def q_step(g, stage):
        gather_step(qbuf, q_s, q_r, g, stage)

    def a_step(g, stage):
        gather_step(abuf, a_s, a_r, g, stage)

    def reduce_copies(g, stage):
        parity = g % 2
        size = 1 << stage
        slot = my_slot(parity)
        other = slot // size * size + (1 - 2 * ((slot // size) % 2)) * size
        away, land = pl.ds(other, size), pl.ds(size, size)
        return (
            remote(osend.at[g, away], orecv.at[g, land], o_s.at[g, stage], o_r.at[g, stage], parity, stage),
            remote(stat.at[g, away], srecv.at[g, land], t_s.at[g, stage], t_r.at[g, stage], parity, stage),
        )

    def reduce_start(g, stage):
        for copy in reduce_copies(g, stage):
            copy.start()

    def reduce_merge(g, stage):
        for copy in reduce_copies(g, stage):
            copy.wait_recv()
        size = 1 << stage
        kept = my_slot(g % 2) // size * size

        def one(i, unused):
            mine, theirs = stat[g, kept + i], srecv[g, size + i]
            peak = jnp.maximum(mine[0:1], theirs[0:1])
            w_mine, w_theirs = jnp.exp2(mine[0:1] - peak), jnp.exp2(theirs[0:1] - peak)
            sums = mine[1:2] * w_mine + theirs[1:2] * w_theirs
            out = o32[g, kept + i] * w_mine + orecv[g, size + i].astype(jnp.float32) * w_theirs
            o32[g, kept + i] = out
            osend[g, kept + i] = out.astype(jnp.bfloat16)
            stat[g, kept + i] = jnp.concatenate(
                [peak, sums, jnp.zeros((6, HD), jnp.float32)], axis=0
            )
            return 0

        lax.fori_loop(0, size, one, 0)

    def finish(g):
        slot = my_slot(g % 2)
        tile = (o32[g, slot] / stat[g, slot][1:2]).T.astype(jnp.bfloat16)
        for h in range(group_size):
            abuf[g, slot, :, h * HD : (h + 1) * HD] = tile[h * rows : (h + 1) * rows]

    def flip(mask):
        out = me
        for b in range(bits):
            if mask >> b & 1:
                out = out + (1 - 2 * ((me // (1 << b)) % 2)) * (1 << b)
        return out

    def flip_slot(slot, delta):
        for b in range(bits):
            if delta >> b & 1:
                slot = slot + (1 - 2 * ((slot // (1 << b)) % 2)) * (1 << b)
        return slot

    def device_at(g, delta):
        order = bit_order(bits, 0 if delta < 4 else g % 2)
        return flip(sum(1 << order[b] for b in range(bits) if delta >> b & 1))

    def direct(src, dst, kind, g, delta, i):
        return pltpu.make_async_remote_copy(
            src_ref=src, dst_ref=dst, send_sem=d_s.at[g, kind, i], recv_sem=d_r.at[g, kind, i],
            device_id=(device_at(g, delta), core), device_id_type=MESH,
        )

    def spread_copies(g, phase):
        size = 1 if phase == 0 else 4
        part = abuf.at[g, pl.ds(my_slot(g % 2) // size * size, size)]
        return [direct(part, part, phase, g, i * size, i - 1) for i in (1, 2, 3)]

    def last_copies(g):
        out = []
        slot = my_slot(g % 2)
        for i in (1, 2, 3):
            away = flip_slot(slot, i)
            out.append(direct(osend.at[g, away], orecv.at[g, i], 2, g, i, i - 1))
            out.append(direct(stat.at[g, away], srecv.at[g, i], 3, g, i, i - 1))
        return out

    def last_merge(g):
        slot = my_slot(g % 2)
        stats = [stat[g, slot]] + [srecv[g, i] for i in (1, 2, 3)]
        peak = functools.reduce(jnp.maximum, [x[0:1] for x in stats])
        weights = [jnp.exp2(x[0:1] - peak) for x in stats]
        outs = [o32[g, slot]] + [orecv[g, i].astype(jnp.float32) for i in (1, 2, 3)]
        sums = sum(x[1:2] * w for x, w in zip(stats, weights))
        o32[g, slot] = sum(o * w for o, w in zip(outs, weights))
        stat[g, slot] = jnp.concatenate([peak, sums, jnp.zeros((6, HD), jnp.float32)], axis=0)

    def start_all(copies):
        for copy in copies:
            copy.start()

    def reduce_next(g):
        reduce_merge(g, 3)
        reduce_start(g, 2)

    def reduce_direct(g):
        reduce_merge(g, 2)
        start_all(last_copies(g))

    def reduce_end(g):
        for copy in last_copies(g):
            copy.wait_recv()
        last_merge(g)
        finish(g)
        start_all(spread_copies(g, 0))

    def a_second(g):
        for copy in spread_copies(g, 0):
            copy.wait_recv()
        gather_copy(abuf, a_s, a_r, g, 2).start()

    events = (
        (0, q_step, 0, 2), (0, q_step, 1, 1), (1, q_step, 0, 3), (2, q_step, 1, 2),
        (3, q_step, 0, 4), (4, q_step, 1, 3), (4, q_step, 2, 0), (6, q_step, 2, 1),
        (7, q_step, 1, 4), (8, reduce_start, 0, 3), (8, q_step, 2, 2), (10, q_step, 2, 3),
        (12, reduce_start, 1, 3), (12, reduce_next, 0), (12, q_step, 3, 0), (14, q_step, 3, 1),
        (15, q_step, 2, 4), (15, reduce_direct, 0), (16, reduce_next, 1), (16, q_step, 3, 2),
        (18, reduce_end, 0), (18, q_step, 3, 3), (19, reduce_direct, 1), (20, reduce_start, 2, 3),
        (20, a_second, 0), (22, reduce_end, 1), (23, q_step, 3, 4), (23, a_step, 0, 3),
        (24, reduce_next, 2), (24, a_second, 1), (26, reduce_direct, 2), (27, a_step, 1, 3),
        (27, a_step, 0, 4), (28, reduce_start, 3, 3), (28, reduce_end, 2), (30, a_second, 2),
        (31, a_step, 1, 4),
    )

    load_v = pltpu.make_async_copy(cv_ref, vbuf, load_sem.at[0])
    load_k = pltpu.make_async_copy(ck_ref, kbuf, load_sem.at[1])
    load_w = pltpu.make_async_copy(w_ref, wbuf, load_sem.at[2])
    load_v.start()
    load_k.start()
    load_w.start()
    barrier = pltpu.get_barrier_semaphore()
    masks = [1 << b for b in range(bits)] + [3, 3 << (bits - 2)]
    for mask in masks:
        pl.semaphore_signal(barrier, inc=1, device_id=(flip(mask), core), device_id_type=MESH)
    pl.semaphore_signal(barrier, inc=1, device_id=(me, 1 - core), device_id_type=MESH)

    def barrier_wait():
        pl.semaphore_wait(barrier, len(masks) + 1)

    cosine, sine = trig_ref[0], trig_ref[1]

    def turned(block):
        x = block.astype(jnp.float32)
        return (x * cosine + pltpu.roll(x, HD // 2, 1) * sine).astype(jnp.bfloat16)

    for g in range(groups):
        slot = my_slot(g % 2)
        for h in range(group_size):
            at = (g * group_size + h) * HD
            qbuf[g, slot, h * rows : (h + 1) * rows] = turned(q_ref[:, at : at + HD])
    barrier_wait()
    for g in range(2):
        q_step(g, 0)
    for g in range(groups):
        knew[:, g * HD : (g + 1) * HD] = turned(kn_ref[:, g * HD : (g + 1) * HD])

    load_v.wait()

    def transpose_values(g):
        def one(i, unused):
            at = pl.ds(pl.multiple_of(i * 512, 512), 512)
            vt[g, 0:HD, at] = vbuf[at, g * HD : (g + 1) * HD].T
            return 0

        lax.fori_loop(0, keys // 512, one, 0)
        fresh = jnp.concatenate(
            [vn_ref[:, g * HD : (g + 1) * HD], jnp.zeros((HD - rows, HD), jnp.bfloat16)], axis=0
        )
        vt[g, 0:HD, keys : keys + HD] = fresh.T
        vt[g, HD : HD + 16, :] = jnp.ones((16, keys + HD), jnp.bfloat16)

    transpose_values(0)
    q_step(0, 1)
    for g in range(1, groups):
        transpose_values(g)
    load_k.wait()

    nt = (((1,), (1,)), ((), ()))

    def query_block(g, rb):
        return qbuf[g, pl.ds(rb * per, per)].reshape(RB, HD)

    def head_lanes(g):
        return pl.ds(pl.multiple_of(g * HD, HD), HD)

    def new_scores(g, rb, slot):
        scores = lax.dot_general(
            knew[:, head_lanes(g)], query_block(g, rb), nt, preferred_element_type=jnp.float32
        )
        cols = pl.ds(pl.multiple_of(rb * RB, RB), RB)
        last = rinfo_ref[g % 2, :, cols]
        first = last - (last & (TURN - 1))
        kpos = kpos_ref[...]
        scores = jnp.where((kpos <= last) & (kpos >= first), scores, -1e30)
        sn_buf[slot] = scores
        return jnp.max(scores.reshape(rows // 8, 8, RB), axis=0)

    def cache_scores(g, rb, kc, slot):
        at = pl.ds(pl.multiple_of(kc * kc_rows, kc_rows), kc_rows)
        scores = lax.dot_general(
            kbuf[at, head_lanes(g)], query_block(g, rb), nt, preferred_element_type=jnp.float32
        )
        s_buf[slot, at, :] = scores
        return jnp.max(scores.reshape(kc_rows // 8, 8, RB), axis=0)

    levels = blocks.bit_length() - 1

    def block_at(g, j):
        first = 1 - jnp.minimum(g, 1)
        mine = my_slot(g % 2) // per
        out = 0
        for b in range(levels):
            same = (mine // (1 << b) + j // (1 << b) + 1 - first) % 2
            out = out + same * (1 << b)
        return out

    start = block_at(0, 0)
    m_buf[...] = lax.fori_loop(
        0, chunks, lambda kc, m: jnp.maximum(m, cache_scores(0, start, kc, 0)),
        new_scores(0, start, 0),
    )
    steps = groups * blocks

    def step(t, unused):
        g, j = t // blocks, t % blocks
        for at, act, *what in events:
            pl.when(t == at)(functools.partial(act, *what))
        rb = block_at(g, j)

        now, later = t % 2, (t + 1) % 2
        after = jnp.minimum(t + 1, steps - 1)
        g2 = after // blocks
        rb2 = block_at(g2, after % blocks)
        peak = jnp.max(m_buf[...], axis=0, keepdims=True) * SCORE_FACTOR
        m0 = new_scores(g2, rb2, later)
        p_new = jnp.exp2(sn_buf[now] * SCORE_FACTOR - peak).astype(jnp.bfloat16)
        p_new = jnp.concatenate([p_new, jnp.zeros((HD - rows, RB), jnp.bfloat16)], axis=0)
        acc = jnp.dot(vt[g, :, keys : keys + HD], p_new, preferred_element_type=jnp.float32)

        def inner(kc, carry):
            m, acc = carry
            at = pl.ds(pl.multiple_of(kc * kc_rows, kc_rows), kc_rows)
            p = jnp.exp2(s_buf[now, at, :] * SCORE_FACTOR - peak).astype(jnp.bfloat16)
            acc = acc + jnp.dot(vt[g, :, at], p, preferred_element_type=jnp.float32)
            return jnp.maximum(m, cache_scores(g2, rb2, kc, later)), acc

        m, acc = lax.fori_loop(0, chunks, inner, (m0, acc))
        m_buf[...] = m
        for i in range(per):
            lanes = slice(i * HD, (i + 1) * HD)
            out = acc[0:HD, lanes]
            o32[g, rb * per + i] = out
            osend[g, rb * per + i] = out.astype(jnp.bfloat16)
            stat[g, rb * per + i] = jnp.concatenate(
                [peak[:, lanes], acc[HD : HD + 1, lanes], jnp.zeros((6, HD), jnp.float32)], axis=0
            )
        return 0

    lax.fori_loop(0, steps, step, 0)

    def project(g):
        part = jnp.dot(
            abuf[g].reshape(n * rows, group_size * HD),
            wbuf[g * group_size * HD : (g + 1) * group_size * HD, :],
            preferred_element_type=jnp.float32,
        )
        proj[g % 2] = part if g < 2 else proj[g % 2] + part

    last = groups - 1
    reduce_next(last)
    load_w.wait()
    project(0)
    a_step(last - 1, 3)
    reduce_direct(last)
    project(1)
    reduce_end(last)
    for g in range(groups):
        att_ref[:, g * group_size * HD : (g + 1) * group_size * HD] = abuf[g, my_slot(g % 2)]
    for copy in spread_copies(last, 0):
        copy.wait_recv()
    start_all(spread_copies(last, 1))
    a_step(last - 1, 4)
    project(last - 1)
    for copy in spread_copies(last, 1):
        copy.wait_recv()
    project(last)
    even, odd = slot_owners(bits, 0), slot_owners(bits, 1)
    for owner in range(n):
        se, so = even.index(owner), odd.index(owner)
        tile = proj[0, se * rows : (se + 1) * rows] + proj[1, so * rows : (so + 1) * rows]
        half, at = owner // (n // 2), owner % (n // 2) * rows
        total[half, at : at + rows] = tile
        hsend[half, at : at + rows] = tile.astype(jnp.bfloat16)
    swap = pltpu.make_async_remote_copy(
        src_ref=hsend.at[1 - core], dst_ref=hrecv, send_sem=h_s, recv_sem=h_r,
        device_id=(me, 1 - core), device_id_type=MESH,
    )
    swap.start()
    swap.wait_recv()
    summed = total[core] + hrecv[...].astype(jnp.float32)
    hid_ref[...] = (res_ref[...].astype(jnp.float32) + summed).astype(jnp.bfloat16)
    swap.wait_send()

    def drain(g, unused):
        for stage in range(bits):
            gather_copy(qbuf, q_s, q_r, g, stage).wait_send()
        for stage in (2, 3):
            for copy in reduce_copies(g, stage):
                copy.wait_send()
        return 0

    def drain_rest(g, unused):
        for stage in (2, 3):
            gather_copy(abuf, a_s, a_r, g, stage).wait_send()
        return 0

    lax.fori_loop(0, groups, drain, 0)
    lax.fori_loop(0, last, drain_rest, 0)
    for g in range(groups):
        for copy in last_copies(g) + spread_copies(g, 0):
            copy.wait_send()
    for copy in spread_copies(last, 1):
        copy.wait_send()


def fused_device(
    n, queries, cache_keys, cache_values, new_keys, new_values, new_pos, residual, out_weight
):
    bits = n.bit_length() - 1
    rows = queries.shape[0]
    keys = cache_keys.shape[0]
    groups = cache_keys.shape[1] // HD
    group_size = queries.shape[1] // cache_keys.shape[1]
    row_start = lax.axis_index("seq") * rows
    own_pos = lax.dynamic_slice_in_dim(new_pos, row_start, rows)
    frequency = jnp.exp(
        (jnp.arange(HD, dtype=jnp.int32) % (HD // 2)).astype(jnp.float32)
        * (-2.0 * math.log(rope_base) / HD)
    )
    angles = (own_pos % TURN).astype(jnp.float32)[:, None] * frequency[None, :]
    sign = jnp.where(jnp.arange(HD) < HD // 2, -1.0, 1.0)
    trig = jnp.stack([jnp.cos(angles), jnp.sin(angles) * sign])
    kpos = jnp.broadcast_to(own_pos[:, None], (rows, RB))
    infos = []
    for parity in (0, 1):
        axes = [bits - 1 - b for b in reversed(bit_order(bits, parity))]
        table = new_pos.reshape((2,) * bits + (rows,)).transpose(*axes, bits).reshape(n, 1, rows)
        infos.append(jnp.broadcast_to(table, (n, group_size, rows)).reshape(1, -1))
    rinfo = jnp.stack(infos)
    bf, f32 = jnp.bfloat16, jnp.float32
    vmem, hbm = pl.BlockSpec(memory_space=pltpu.VMEM), pl.BlockSpec(memory_space=pl.ANY)
    sems = pltpu.SemaphoreType.DMA((groups, bits))
    width = out_weight.shape[1]
    half = n * rows // 2
    return pl.pallas_call(
        functools.partial(fused_kernel, bits, groups, group_size, rows),
        out_shape=(
            jax.ShapeDtypeStruct(queries.shape, bf),
            jax.ShapeDtypeStruct(residual.shape, bf),
        ),
        in_specs=[vmem] * 6 + [hbm] * 3 + [vmem],
        out_specs=(vmem, vmem),
        scratch_shapes=[
            pltpu.VMEM(cache_keys.shape, bf),
            pltpu.VMEM(cache_values.shape, bf),
            pltpu.VMEM(out_weight.shape, bf),
            pltpu.VMEM((groups, HD + 16, keys + HD), bf),
            pltpu.VMEM((2, keys, RB), f32),
            pltpu.VMEM((2, rows, RB), f32),
            pltpu.VMEM((8, RB), f32),
            pltpu.VMEM((groups, n, HD, HD), bf),
            pltpu.VMEM((groups, n, HD, HD), f32),
            pltpu.VMEM((groups, n, 8, HD), f32),
            pltpu.VMEM((groups, n, HD, HD), bf),
            pltpu.VMEM((groups, n, HD, HD), bf),
            pltpu.VMEM((groups, n, 8, HD), f32),
            pltpu.VMEM((groups, n, rows, group_size * HD), bf),
            pltpu.VMEM((2, n * rows, width), f32),
            pltpu.VMEM((2, half, width), f32),
            pltpu.VMEM((2, half, width), bf),
            pltpu.VMEM((half, width), bf),
            pltpu.VMEM(new_keys.shape, bf),
            pltpu.SemaphoreType.DMA((3,)),
            sems, sems, sems, sems, sems, sems, sems, sems,
            pltpu.SemaphoreType.DMA,
            pltpu.SemaphoreType.DMA,
            pltpu.SemaphoreType.DMA((groups, 4, 3)),
            pltpu.SemaphoreType.DMA((groups, 4, 3)),
        ],
        compiler_params=pltpu.CompilerParams(
            collective_id=0, has_side_effects=True, vmem_limit_bytes=60 * 2**20
        ),
    )(
        queries, new_keys, new_values, trig, kpos, rinfo,
        cache_keys, cache_values, out_weight, residual,
    )


def on_device(n, *arrays):
    queries, cache_keys = arrays[0], arrays[1]
    rows, keys = queries.shape[0], cache_keys.shape[0]
    groups = cache_keys.shape[1] // HD
    group_size = queries.shape[1] // cache_keys.shape[1]
    fits = n == 16 and groups == 4 and rows == 32 and group_size * rows == HD and keys % KC == 0
    if fits and keys == 4096:
        return fused_device(n, *arrays)
    return plain_device(*arrays)


def solution(mesh):
    return jax.shard_map(
        functools.partial(on_device, mesh.shape["seq"]),
        mesh=mesh,
        in_specs=(
            P("seq", "head"),
            P("seq", "head"),
            P("seq", "head"),
            P("seq", "head"),
            P("seq", "head"),
            P(),
            P("head", "seq"),
            P("head", "seq"),
        ),
        out_specs=(P("seq", "head"), P("head", "seq")),
        check_vma=False,
    )
```
